32 devices in a mesh: groups: 2 (over y), patch: 8 (over z, x), member: 2 (over core).
Axes of the slice: x: 2, y: 2, z: 4, core: 2. Of those that a mesh axis runs over, the one named last changes fastest.
Arguments:
- fields: bfloat16 [8, 16384, 84], P(('groups', 'member'), 'patch'), parts along dimension 0, may hold values from -6 to 6
- w_embed: bfloat16 [84, 512], replicated, may hold values from -0.625 to 0.625
- b_embed: float32 [512], replicated, may hold values from -3 to 3
- w_encode: bfloat16 [512, 512], replicated, may hold values from -0.25 to 0.25
- b_encode: float32 [512], replicated, may hold values from -3 to 3
- mesh_gain: float32 [512], replicated, may hold values from 0.1 to 1.9
- w_receive: bfloat16 [512, 512], replicated, may hold values from -0.25 to 0.25
- w_sender: bfloat16 [512, 512], replicated, may hold values from -0.25 to 0.25
- b_process: float32 [512], replicated, may hold values from -3 to 3
- w_update: bfloat16 [512, 512], replicated, may hold values from -0.25 to 0.25
- w_decmesh: bfloat16 [512, 512], replicated, may hold values from -0.25 to 0.25
- w_decgrid: bfloat16 [512, 512], replicated, may hold values from -0.25 to 0.25
- b_decode: float32 [512], replicated, may hold values from -3 to 3
- w_output: bfloat16 [512, 84], replicated, may hold values from -0.25 to 0.25
- b_output: float32 [84], replicated, may hold values from -3 to 3
- g2m_senders: int32 [2048, 16], P('patch'), may hold values from -1 to 16383, as said below
- m2g_senders: int32 [16384, 3], P('patch'), may hold values from 0 to 2047, as said below
- mesh_neighbours: int32 [2048, 6], P('patch'), may hold values from 0 to 2047, as said below
- climatology: bfloat16 [16384, 84], P('patch'), may hold values from -6 to 6
- week_sum: float32 [32768, 84], P(('groups', 'patch')), parts along dimension 0, may hold values from -6 to 6
Outputs:
- prediction: bfloat16 [8, 16384, 84], P(('groups', 'member'), 'patch'), parts along dimension 0
- week_total: float32 [32768, 84], P(('groups', 'patch')), parts along dimension 0
The draws below stay inside these ranges and needn't reach their ends.
There are 2 independent parts, one for each index of `groups`. The reference program is written for one: setup_inputs(seed, part) draws one part's arguments, and reference() takes and returns one part's arrays. A program takes and returns all parts, laid end to end along the dimension named above; an argument that names none is the same for every part. Nothing has to cross between parts.
Inputs may be any that keep to these rules, and one draw needn't show every extreme that they name: `g2m_senders`: for mesh node n = p * 256 + r (0 <= r < 256) every used slot holds (p * 2048 + r * 8 + k) modulo 16384 with -128 <= k <= 135; both ends of k occur in every draw. Used slots come first, -1 marks empty ones; a mesh node has 8 to 16 used slots, and some mesh node has all 16 in every draw. `m2g_senders`: for grid node g = p * 2048 + r (0 <= r < 2048) every entry is (p * 256 + r // 8 + k) modulo 2048 with -32 <= k <= 32; both ends of k occur in every draw. `mesh_neighbours`: every neighbour of mesh node n is (n + k) modulo 2048 with 1 <= |k| <= 32; both k = 32 and k = -32 occur in every draw.
All inputs are finite; a program needn't handle non-finite values.
Results may differ from the reference program's by a relative error of at most 0.008.
Values may be sent and summed in bfloat16 or wider, within the bound.
No kernel may reach another device: no remote copies, remote signals or barrier semaphores. Data moves between devices by JAX's collectives and lax.ppermute only.
A program may use at most 128 MiB of HBM per device.

```python
import jax
import jax.numpy as jnp
from jax import lax

CHAN = 84
HID = 512
G_DEV = 2048
M_DEV = 256
K_ENC = 16
TRI = 3
NBRS = 6
REACH = 32
GRIM = 128
PATCHES = 8
GRID = 16384
MESH = 2048
MEMBERS = 4


def draw_g2m_senders(key, part):
    key = jax.random.fold_in(key, 21)
    count_key, offset_key, pick_key = jax.random.split(key, 3)
    stride = G_DEV // M_DEV
    nodes = jnp.arange(MESH)[:, None]
    slot = jnp.arange(K_ENC)[None, :]
    counts = jax.random.randint(count_key, (MESH, 1), K_ENC // 2, K_ENC + 1)
    chosen = jax.random.randint(pick_key, (), 0, MESH)
    counts = jnp.where(nodes == chosen, K_ENC, counts)
    offsets = jax.random.randint(offset_key, (MESH, K_ENC), -GRIM, stride + GRIM)
    offsets = jnp.where((nodes == chosen) & (slot == 0), -GRIM, offsets)
    offsets = jnp.where((nodes == chosen) & (slot == 1), stride + GRIM - 1, offsets)
    centre = nodes // M_DEV * G_DEV + nodes % M_DEV * stride
    senders = jnp.mod(centre + offsets, GRID)
    return jnp.where(slot < counts, senders, -1).astype(jnp.int32)


def draw_m2g_senders(key, part):
    key = jax.random.fold_in(key, 22)
    offset_key, pick_key = jax.random.split(key, 2)
    stride = G_DEV // M_DEV
    nodes = jnp.arange(GRID)[:, None]
    slot = jnp.arange(TRI)[None, :]
    offsets = jax.random.randint(offset_key, (GRID, TRI), -REACH, REACH + 1)
    chosen = jax.random.randint(pick_key, (), 0, GRID)
    offsets = jnp.where((nodes == chosen) & (slot == 0), -REACH, offsets)
    offsets = jnp.where((nodes == chosen) & (slot == 1), REACH, offsets)
    centre = nodes // G_DEV * M_DEV + nodes % G_DEV // stride
    return jnp.mod(centre + offsets, MESH).astype(jnp.int32)


def draw_mesh_neighbours(key, part):
    key = jax.random.fold_in(key, 13)
    length_key, sign_key, pick_key = jax.random.split(key, 3)
    lengths = jax.random.randint(length_key, (MESH, NBRS), 1, REACH + 1)
    signs = jax.random.randint(sign_key, (MESH, NBRS), 0, 2) * 2 - 1
    first_pick = jax.random.randint(pick_key, (), 0, MESH * NBRS)
    second_pick = (first_pick + 1) % (MESH * NBRS)
    flat = jnp.arange(MESH * NBRS).reshape(MESH, NBRS)
    offsets = lengths * signs
    offsets = jnp.where(flat == first_pick, REACH, jnp.where(flat == second_pick, -REACH, offsets))
    return jnp.mod(jnp.arange(MESH)[:, None] + offsets, MESH).astype(jnp.int32)


def levels(rng, shape, cuts, low, top_value):
    def one(axis_at, shards_of):
        draws = jax.random.uniform(jax.random.fold_in(jax.random.fold_in(rng, 6), axis_at), (shards_of,), jnp.float32, low / len(cuts), top_value / len(cuts))
        return jnp.repeat(jnp.exp(draws), shape[axis_at] // shards_of).reshape((-1,) + (1,) * (len(shape) - axis_at - 1))

    level = one(*cuts[0])
    for cut in cuts[1:]:
        level = level * one(*cut)
    return level


def bell_draw(key, shape, deviation, reach, cuts=(), kind=jnp.bfloat16):
    drawn = deviation * jax.random.normal(key, shape, jnp.float32)
    if cuts:
        drawn = drawn * levels(key, shape, cuts, -0.22, 0.18)
    return jnp.clip(drawn, -reach, reach).astype(kind)


def setup_inputs(seed: int = 0, part: int = 0) -> dict:
    key_of = jax.random.split(jax.random.key(seed), 21)
    part_splits = jax.random.split(jax.random.fold_in(key_of[20], part), 21)
    fields = bell_draw(part_splits[0], (MEMBERS, GRID, CHAN), 1.0, 6.0, ((0, 2), (1, 8)))
    w_embed = bell_draw(key_of[1], (CHAN, HID), CHAN ** -0.5, 0.625)
    b_embed = bell_draw(key_of[2], (HID,), 0.5, 3.0, (), jnp.float32)
    w_encode = bell_draw(key_of[3], (HID, HID), HID ** -0.5, 0.25)
    b_encode = bell_draw(key_of[4], (HID,), 0.5, 3.0, (), jnp.float32)
    mesh_gain = jnp.clip(1.0 + 0.18 * jax.random.normal(key_of[5], (HID,), jnp.float32), 0.1, 1.9)
    w_receive = bell_draw(key_of[6], (HID, HID), HID ** -0.5, 0.25)
    w_sender = bell_draw(key_of[7], (HID, HID), HID ** -0.5, 0.25)
    b_process = bell_draw(key_of[8], (HID,), 0.5, 3.0, (), jnp.float32)
    w_update = bell_draw(key_of[9], (HID, HID), HID ** -0.5, 0.25)
    w_decmesh = bell_draw(key_of[10], (HID, HID), HID ** -0.5, 0.25)
    w_decgrid = bell_draw(key_of[11], (HID, HID), HID ** -0.5, 0.25)
    b_decode = bell_draw(key_of[12], (HID,), 0.5, 3.0, (), jnp.float32)
    w_output = bell_draw(key_of[13], (HID, CHAN), HID ** -0.5, 0.25)
    b_output = bell_draw(key_of[14], (CHAN,), 0.5, 3.0, (), jnp.float32)
    g2m_senders = draw_g2m_senders(jax.random.fold_in(key_of[20], 71), part)
    m2g_senders = draw_m2g_senders(jax.random.fold_in(key_of[20], 71), part)
    mesh_neighbours = draw_mesh_neighbours(jax.random.fold_in(key_of[20], 71), part)
    climatology = bell_draw(key_of[18], (GRID, CHAN), 1.0, 6.0, ((0, 8),))
    week_sum = bell_draw(part_splits[19], (GRID, CHAN), 1.0, 6.0, ((0, 8),), jnp.float32)
    return {"fields": fields, "w_embed": w_embed, "b_embed": b_embed, "w_encode": w_encode, "b_encode": b_encode, "mesh_gain": mesh_gain, "w_receive": w_receive, "w_sender": w_sender, "b_process": b_process, "w_update": w_update, "w_decmesh": w_decmesh, "w_decgrid": w_decgrid, "b_decode": b_decode, "w_output": w_output, "b_output": b_output, "g2m_senders": g2m_senders, "m2g_senders": m2g_senders, "mesh_neighbours": mesh_neighbours, "climatology": climatology, "week_sum": week_sum}


def rounded(values):
    return lax.optimization_barrier(values.astype(jnp.bfloat16)).astype(jnp.float32)

def encode(messages, senders):
    blocks = senders.reshape(PATCHES, M_DEV, K_ENC)

    def one_patch(ids):
        rows = jnp.take(messages, jnp.maximum(ids, 0).reshape(-1).astype(jnp.int32), axis=0)
        rows = rows.reshape(M_DEV, K_ENC, HID).astype(jnp.float32)
        rows = jnp.where((ids >= 0)[:, :, None], rows, jnp.zeros_like(rows))
        return lax.optimization_barrier(jnp.sum(rows, axis=1))
    return lax.map(one_patch, blocks).reshape(MESH, HID)

def decode(mesh_part, grid_latent, senders, w_decgrid, b_decode):
    latents = grid_latent.reshape(PATCHES, G_DEV, HID)
    blocks = senders.reshape(PATCHES, G_DEV, TRI)

    def one_patch(pieces):
        latent_rows, ids = pieces
        grid_part = jnp.dot(latent_rows, w_decgrid, preferred_element_type=jnp.float32) + b_decode
        total = jnp.zeros((G_DEV, HID), jnp.float32)
        for column in range(TRI):
            total = total + rounded(jax.nn.silu(jnp.take(mesh_part, ids[:, column], axis=0) + grid_part))
        return total.astype(jnp.bfloat16)
    return lax.map(one_patch, (latents, blocks)).reshape(GRID, HID)

def reference(fields, w_embed, b_embed, w_encode, b_encode, mesh_gain, w_receive, w_sender, b_process, w_update, w_decmesh, w_decgrid, b_decode, w_output, b_output, g2m_senders, m2g_senders, mesh_neighbours, climatology, week_sum):
    predictions = []
    for member in range(MEMBERS):
        state_rows = fields[member]
        grid_latent = jax.nn.silu(jnp.dot(state_rows, w_embed, preferred_element_type=jnp.float32) + b_embed).astype(jnp.bfloat16)
        messages = jax.nn.silu(jnp.dot(grid_latent, w_encode, preferred_element_type=jnp.float32) + b_encode).astype(jnp.bfloat16)
        mesh_sum = encode(messages, g2m_senders)
        scale = lax.rsqrt(lax.optimization_barrier(jnp.mean(mesh_sum * mesh_sum, axis=-1, keepdims=True)) + 1e-05)
        mesh_latent = (mesh_gain * mesh_sum * scale).astype(jnp.bfloat16)
        sender_part = jnp.dot(mesh_latent, w_sender, preferred_element_type=jnp.float32)
        receiver_part = jnp.dot(mesh_latent, w_receive, preferred_element_type=jnp.float32) + b_process
        process_total = jnp.zeros((MESH, HID), jnp.float32)
        for column in range(NBRS):
            process_total = process_total + jax.nn.silu(receiver_part + jnp.take(sender_part, mesh_neighbours[:, column], axis=0))
        process_sum = process_total.astype(jnp.bfloat16)
        mesh_new = (mesh_latent.astype(jnp.float32) + jnp.dot(process_sum, w_update, preferred_element_type=jnp.float32)).astype(jnp.bfloat16)
        mesh_part = jnp.dot(mesh_new, w_decmesh, preferred_element_type=jnp.float32)
        grid_sum = decode(mesh_part, grid_latent, m2g_senders, w_decgrid, b_decode)
        delta = jnp.dot(grid_sum, w_output, preferred_element_type=jnp.float32) + b_output
        predictions.append((state_rows.astype(jnp.float32) + delta).astype(jnp.bfloat16))
    prediction = jnp.stack(predictions, axis=0)
    ensemble = lax.optimization_barrier(jnp.sum(prediction.astype(jnp.float32), axis=0)) / MEMBERS
    week_total = week_sum + ensemble - climatology.astype(jnp.float32)
    return (prediction, week_total)
```

```python
import functools

import jax
import jax.numpy as jnp
from jax import lax
from jax.experimental import pallas as pl
from jax.experimental.pallas import tpu as pltpu
from jax.sharding import PartitionSpec as P

REACH = 32
GRIM = 128
MHALO = 2 * REACH
EMPTY = -4096
F32 = jnp.float32
BF16 = jnp.bfloat16


def dot(a, b):
    return jnp.dot(a, b, preferred_element_type=F32)


def silu(u):
    return u + u * jnp.tanh(u)


def iota(shape, dim):
    return lax.broadcasted_iota(jnp.int32, shape, dim)


def ranks(shape, dim):
    return iota(shape, dim).astype(F32).astype(BF16)


def twice(a):
    return jnp.concatenate([a, a], axis=0)


def wide(a, width):
    return jnp.concatenate([a] * (width // a.shape[1]), axis=1)


def wrap(a, size):
    a = jnp.where(a < 0, a + size, a)
    return jnp.where(a >= size, a - size, a)


def small(idx):
    return idx.astype(F32).astype(BF16)


def marks(idx, height):
    rows = ranks((height, idx.shape[1]), 0)
    return jnp.where(rows == idx, jnp.ones((), BF16), jnp.zeros((), BF16))


def counts(idx, height, base):
    parts = []
    for first in range(0, height, 256):
        size = min(256, height - first)
        near = small(idx - (base + first))
        total = marks(near[0:1], size)
        for slot in range(1, idx.shape[0]):
            total = total + marks(near[slot : slot + 1], size)
        parts.append(total)
    return parts[0] if len(parts) == 1 else jnp.concatenate(parts, axis=0)


def spread(channels, members, member):
    shape = (channels * members, channels)
    return jnp.where(iota(shape, 0) == iota(shape, 1) * members + member, 1.0, 0.0).astype(BF16)


def turned(w, scale):
    return (w.astype(F32) * scale).T.astype(BF16)


def column(b, scale):
    return (jnp.broadcast_to(b, (128, b.shape[1])) * scale).T


def fetch(sources, targets, sems):
    copies = [
        pltpu.make_async_copy(source, target, sems.at[i])
        for i, (source, target) in enumerate(zip(sources, targets))
    ]
    for copy in copies:
        copy.start()
    return copies


def pack_kernel(
    patches,
    place,
    fields_hbm,
    senders_hbm,
    near_hbm,
    x_ref,
    up_ref,
    down_ref,
    k_ref,
    n_ref,
    fields_ref,
    senders_ref,
    near_ref,
    sems,
):
    copies = fetch(
        (fields_hbm, senders_hbm, near_hbm), (fields_ref, senders_ref, near_ref), sems
    )
    for copy in copies:
        copy.wait()
    channels, members, rows = fields_ref.shape
    nodes = senders_ref.shape[1]
    nbrs = near_ref.shape[0]
    stride = rows // nodes
    halo = up_ref.shape[1]
    kx = channels * members
    x = fields_ref[...].reshape(kx, rows)
    x_ref[:kx, :] = x
    x_ref[kx:, :] = jnp.zeros((x_ref.shape[0] - kx, rows), BF16)
    senders = senders_ref[...]
    node = iota(senders.shape, 1)
    k = wrap(senders - place[0] * rows - node * stride + GRIM, rows * patches) - GRIM
    k = jnp.where(senders >= 0, k, EMPTY)
    k = pltpu.roll(k, MHALO, 1)
    k_ref[...] = k
    near = near_ref[...]
    near = wrap(near - place[0] * nodes - iota(near.shape, 1) + REACH, nodes * patches) - REACH
    n_ref[:nbrs, :] = near
    n_ref[nbrs:, :] = jnp.zeros((8 - nbrs, nodes), jnp.int32)
    near = pltpu.roll(n_ref[...], MHALO, 1)
    n_ref[...] = near
    zero = jnp.zeros((8, halo - 3 * 128), F32)
    k = k.astype(F32)[:, :128]
    extra = [k[:8], k[8:], near.astype(F32)[:, :128], zero]
    extra = jnp.concatenate(extra, axis=1).astype(BF16)
    up_ref[...] = jnp.concatenate([x[:, rows - halo :], extra], axis=0)
    down_ref[...] = jnp.concatenate([x[:, :halo], extra], axis=0)


def own_kernel(members, x_ref, k_ref, *refs):
    sources = refs[:13]
    gp_ref, edge_ref, part_ref, embed_t, mesh_t, out_t, encode_t, cols_ref = refs[13:21]
    wcat, bdec = refs[21:23]
    targets, sems = refs[23:36], refs[36]
    copies = fetch(sources, targets, sems)
    for copy in copies:
        copy.wait()
    (
        w_embed,
        b_embed,
        w_encode,
        b_encode,
        gain,
        w_receive,
        w_sender,
        b_process,
        w_update,
        w_decmesh,
        w_decgrid,
        b_decode,
        w_output,
    ) = targets
    channels, hidden = w_embed.shape
    rows = x_ref.shape[1]
    nodes = k_ref.shape[1]
    kx = channels * members
    for m in range(members):
        sp = spread(channels, members, m)
        we = dot(sp, w_embed[...]) * 0.5
        we = jnp.concatenate([we, jnp.zeros((x_ref.shape[0] - kx, hidden), F32)], axis=0)
        embed_t[m * hidden : (m + 1) * hidden, :] = we.T.astype(BF16)
        out_t[:, m * hidden : (m + 1) * hidden] = dot(sp, w_output[...]).astype(BF16)
    enc = turned(w_encode[...], 0.5)
    encode_t[...] = enc
    wcat[:hidden, :] = enc
    wcat[hidden:, :] = turned(w_decgrid[...], 0.5)
    mesh_t[0] = turned(w_sender[...], 0.5)
    mesh_t[1] = turned(w_receive[...], 0.5)
    mesh_t[2] = turned(w_update[...], 1.0)
    mesh_t[3] = turned(w_decmesh[...], 0.5)
    cols_ref[0] = column(b_embed[...], 0.5)
    cols_ref[1] = column(b_encode[...], 0.5)
    cols_ref[2] = column(b_process[...], 0.5)
    cols_ref[3] = column(gain[...], 1.0)
    bdec[...] = column(b_decode[...], 0.5)
    part_ref[...] = jnp.zeros_like(part_ref)
    block = 512
    steps = rows // block

    def step(i, carry):
        o = pl.multiple_of(i * block, block)
        lanes = pl.ds(o, block)
        pre = dot(embed_t[...], x_ref[:, lanes])
        h = silu((pre + wide(twice(cols_ref[0]), block)).astype(BF16))
        msgs = []
        for m in range(members):
            y = dot(wcat[...], h[m * hidden : (m + 1) * hidden, :])
            msgs.append(silu((y[:hidden] + wide(cols_ref[1], block)).astype(BF16)))
            gp_ref[m * hidden : (m + 1) * hidden, lanes] = (
                y[hidden:] + wide(bdec[...], block)
            ).astype(BF16)
        msg = jnp.concatenate(msgs, axis=0)

        @pl.when(i == 0)
        def _():
            edge_ref[:, :GRIM] = msg[:, :GRIM]

        @pl.when(i == steps - 1)
        def _():
            edge_ref[:, GRIM:] = msg[:, block - GRIM :]

        node = (iota(k_ref.shape, 1) + (nodes - MHALO)) % nodes
        idx = k_ref[...] + node * (rows // nodes)
        part_ref[...] += dot(msg, counts(idx, block, o))
        return carry

    lax.fori_loop(0, steps, step, 0)


def rest_kernel(
    members,
    patches,
    place,
    lo_ref,
    hi_ref,
    x_ref,
    k_ref,
    near_ref,
    sent_ref,
    gp_ref,
    edge_ref,
    part_ref,
    embed_t,
    mesh_t,
    out_t,
    encode_t,
    cols_ref,
    bout_ref,
    pred_ref,
    total_ref,
    xh_ref,
    msg_ref,
    sr_ref,
    sent_s,
    p_ref,
):
    hidden = encode_t.shape[0]
    kx = out_t.shape[0]
    channels = kx // members
    rows = x_ref.shape[1]
    halo = lo_ref.shape[1]
    both = members * hidden
    nodes = k_ref.shape[1]
    top = lo_ref.shape[0]
    xh_ref[:top, :halo] = lo_ref[...]
    xh_ref[:top, halo:] = hi_ref[...]
    xh_ref[top:, :] = jnp.zeros((xh_ref.shape[0] - top, 2 * halo), BF16)
    block = 256

    def halo_step(i, carry):
        lanes = pl.ds(pl.multiple_of(i * block, block), block)
        pre = dot(embed_t[...], xh_ref[:, lanes])
        h = silu((pre + wide(twice(cols_ref[0]), block)).astype(BF16))
        for m in range(members):
            y = dot(encode_t[...], h[m * hidden : (m + 1) * hidden, :])
            msg_ref[m * hidden : (m + 1) * hidden, lanes] = silu(
                (y + wide(cols_ref[1], block)).astype(BF16)
            )
        return carry

    lax.fori_loop(0, 2 * halo // block, halo_step, 0)
    tail = kx // 16 * 16
    lo_x = lo_ref[tail : tail + 16, :].astype(F32)[kx - tail :].astype(jnp.int32)
    hi_x = hi_ref[tail : tail + 16, :].astype(F32)[kx - tail :].astype(jnp.int32)
    slots = jnp.concatenate([lo_x[:, :128], lo_x[:, 128:256]], axis=0)
    lane = iota(slots.shape, 1)
    seam = k_ref[:, :128]
    near_by = lane * 8 + (halo - 8 * MHALO)
    own = near_by + seam
    left = jnp.where(lane < MHALO, near_by + slots, jnp.where(own < halo, own, EMPTY))
    slots = jnp.concatenate([hi_x[:, :128], hi_x[:, 128:256]], axis=0)
    near_by = lane * 8 - (rows - GRIM - 8 * (nodes - MHALO))
    own = near_by + seam
    right = jnp.where(lane >= MHALO, near_by + slots, jnp.where(own >= GRIM, own, EMPTY))
    lsum = dot(msg_ref[:, :halo], counts(left, halo, 0)) + dot(
        edge_ref[:, :GRIM], counts(left, GRIM, halo)
    )
    rsum = dot(edge_ref[:, GRIM:], counts(right, GRIM, 0)) + dot(
        msg_ref[:, halo:], counts(right, halo, GRIM)
    )
    seam = part_ref[:, :128]
    lane = iota(seam.shape, 1)
    lsum = lsum + jnp.where(lane >= MHALO, seam, 0.0)
    rsum = rsum + jnp.where(lane < MHALO, seam, 0.0)
    sums = jnp.concatenate([lsum, part_ref[:, 128:], rsum], axis=1)
    ext = sums.shape[1]
    latents = []
    for m in range(members):
        s = sums[m * hidden : (m + 1) * hidden]
        scale = lax.rsqrt(jnp.sum(s * s, axis=0, keepdims=True) * (1.0 / hidden) + 1e-5)
        latents.append((wide(cols_ref[3], ext) * s * scale).astype(BF16))
    latent = jnp.concatenate(latents, axis=1)
    send = dot(mesh_t[0], latent).astype(BF16)
    recv = (dot(mesh_t[1], latent) + wide(cols_ref[2], members * ext)).astype(BF16)
    for m in range(members):
        sr_ref[m * hidden : (m + 1) * hidden, :] = send[:, m * ext : (m + 1) * ext]
    seam = near_ref[:, :128]
    lane = iota(seam.shape, 1)
    blocks = (
        (jnp.where(lane < MHALO, lo_x[:, 256:384], seam), 0, 256),
        (near_ref[:, 128:], 0, 384),
        (jnp.where(lane >= MHALO, hi_x[:, 256:384], seam), 128, 256),
    )
    sums = []
    for b, (k, first, height) in enumerate(blocks):
        at = k + lane + (128 * b - first)
        base = jnp.concatenate(
            [recv[:, m * ext + 128 * b : m * ext + 128 * (b + 1)] for m in range(members)], axis=0
        )
        total = None
        for j in range(0, 6, 2):
            pair = jnp.concatenate([at[j : j + 1], at[j + 1 : j + 2]], axis=1)
            hot = [marks(small(pair - f), min(256, height - f)) for f in range(0, height, 256)]
            hot = hot[0] if len(hot) == 1 else jnp.concatenate(hot, axis=0)
            got = dot(sr_ref[:, first : first + height], hot).astype(BF16) + wide(base, 256)
            act = silu(got).astype(F32)
            act = act[:, :128] + act[:, 128:]
            total = act if total is None else total + act
        sums.append(total.astype(BF16))
    process = jnp.concatenate(
        [s[m * hidden : (m + 1) * hidden] for m in range(members) for s in sums], axis=1
    )
    new = (latent.astype(F32) + dot(mesh_t[2], process)).astype(BF16)
    part = dot(mesh_t[3], new).astype(BF16)
    for m in range(members):
        sr_ref[m * hidden : (m + 1) * hidden, :] = part[:, m * ext : (m + 1) * ext]
    sent = wrap(sent_ref[...] - place[0] * nodes + MHALO, nodes * patches)
    half = rows // 2
    sent_s[...] = jnp.where(iota(sent.shape, 1) >= half, sent - 128, sent).astype(F32)
    shape = (channels, x_ref.shape[0])
    fold = jnp.where(iota(shape, 1) // members == iota(shape, 0), 1.0, 0.0).astype(BF16)
    bout = (iota((kx, channels), 0) // members == iota((kx, channels), 1)).astype(F32)
    bout = jnp.sum(bout * bout_ref[...], axis=1, keepdims=True)
    bout = jnp.broadcast_to(bout, (kx, block))
    p_ref[kx:, :] = jnp.zeros((p_ref.shape[0] - kx, block), BF16)
    for b in range(2):

        def step(i, carry, b=b):
            lanes = pl.ds(pl.multiple_of(b * half + i * block, block), block)
            window = sr_ref[:, 128 * b : 128 * b + 256]
            idx = sent_s[:, lanes].astype(BF16)
            gp = gp_ref[:, lanes]
            total = None
            for j in range(idx.shape[0]):
                act = silu(dot(window, marks(idx[j : j + 1], 256)).astype(BF16) + gp)
                total = act if total is None else total + act
            delta = dot(out_t[...], total) + bout
            pred = (x_ref[:kx, lanes].astype(F32) + delta).astype(BF16)
            pred_ref[:, :, lanes] = pred.reshape(channels, members, block)
            p_ref[:kx, :] = pred
            total_ref[:, lanes] = dot(fold, p_ref[...]).astype(BF16)
            return carry

        lax.fori_loop(0, half // block, step, 0)


def week_kernel(count, total_ref, other_ref, week_ref, clim_ref, out_ref):
    ensemble = (total_ref[...].astype(F32) + other_ref[...].astype(F32)) * (1.0 / count)
    out_ref[...] = week_ref[...] + ensemble - clim_ref[...].astype(F32)


def call(kernel, outs, scratch, name, args, flops, spaces, limit=24):
    kinds = {"s": pltpu.SMEM, "v": pltpu.VMEM, "h": pltpu.HBM}
    args = [
        a if kind == "s" else pltpu.with_memory_space_constraint(a, kinds[kind])
        for a, kind in zip(args, spaces, strict=True)
    ]
    return pl.pallas_call(
        kernel,
        out_shape=outs,
        in_specs=[pl.BlockSpec(memory_space=kinds[kind]) for kind in spaces],
        out_specs=[pl.BlockSpec(memory_space=pltpu.VMEM)] * len(outs),
        scratch_shapes=scratch,
        name=name,
        compiler_params=pltpu.CompilerParams(vmem_limit_bytes=limit * 1024 * 1024),
        cost_estimate=pl.CostEstimate(flops=flops, bytes_accessed=1 << 22, transcendentals=0),
    )(*args)


def copies_of(args):
    return [pltpu.VMEM(a.shape, a.dtype) for a in args] + [pltpu.SemaphoreType.DMA((len(args),))]


def shards(
    fields,
    w_embed,
    b_embed,
    w_encode,
    b_encode,
    mesh_gain,
    w_receive,
    w_sender,
    b_process,
    w_update,
    w_decmesh,
    w_decgrid,
    b_decode,
    w_output,
    b_output,
    g2m_senders,
    m2g_senders,
    mesh_neighbours,
    climatology,
    week_sum,
):
    members, rows, channels = fields.shape
    hidden = w_encode.shape[0]
    nodes, nbrs = mesh_neighbours.shape
    slots = g2m_senders.shape[1]
    patches = lax.axis_size("patch")
    place = lax.axis_index("patch").astype(jnp.int32).reshape(1)
    kx = members * channels
    kpad = -(-kx // 256) * 256
    halo = MHALO * (rows // nodes) + GRIM
    ext = nodes + 2 * MHALO
    shape = jax.ShapeDtypeStruct
    inside = pltpu.VMEM

    args = (jnp.transpose(fields, (2, 0, 1)), g2m_senders.T, mesh_neighbours.T)
    x, from_low, from_high, k, near = call(
        functools.partial(pack_kernel, patches),
        [
            inside((kpad, rows), BF16),
            shape((kx + 8, halo), BF16),
            shape((kx + 8, halo), BF16),
            inside((slots, nodes), jnp.int32),
            inside((8, nodes), jnp.int32),
        ],
        copies_of(args),
        "pack_halo",
        (place,) + args,
        10**7,
        "shhh",
    )
    up = [(i, (i + 1) % patches) for i in range(patches)]
    down = [(target, source) for source, target in up]
    lo = lax.ppermute(from_low, "patch", up)
    hi = lax.ppermute(from_high, "patch", down)

    args = (
        w_embed,
        b_embed[None],
        w_encode,
        b_encode[None],
        mesh_gain[None],
        w_receive,
        w_sender,
        b_process[None],
        w_update,
        w_decmesh,
        w_decgrid,
        b_decode[None],
        w_output.T,
    )
    own = call(
        functools.partial(own_kernel, members),
        [
            inside((members * hidden, rows), BF16),
            inside((members * hidden, 2 * GRIM), BF16),
            inside((members * hidden, nodes), F32),
            inside((members * hidden, kpad), BF16),
            inside((4, hidden, hidden), BF16),
            inside((kx, members * hidden), BF16),
            inside((hidden, hidden), BF16),
            inside((4, hidden, 128), F32),
        ],
        [pltpu.VMEM((2 * hidden, hidden), BF16), pltpu.VMEM((hidden, 128), F32)]
        + copies_of(args),
        "own_rows",
        (x, k) + args,
        10**10,
        "vv" + "h" * len(args),
    )
    pred, total = call(
        functools.partial(rest_kernel, members, patches),
        [shape((channels, members, rows), BF16), shape((channels, rows), BF16)],
        [
            pltpu.VMEM((kpad, 2 * halo), BF16),
            pltpu.VMEM((members * hidden, 2 * halo), BF16),
            pltpu.VMEM((members * hidden, ext), BF16),
            pltpu.VMEM((m2g_senders.shape[1], rows), F32),
            pltpu.VMEM((kpad, 256), BF16),
        ],
        "halo_mesh_decode",
        (place, lo, hi, x, k, near, m2g_senders.T) + tuple(own) + (b_output[None],),
        2 * 10**10,
        "s" + "v" * 15,
    )
    prediction = jnp.transpose(pred, (1, 2, 0))
    other = lax.ppermute(total, "member", [(0, 1), (1, 0)])
    (week_total,) = call(
        functools.partial(week_kernel, members * lax.axis_size("member")),
        [shape((channels, rows), F32)],
        [],
        "week",
        (total, other, week_sum.T, climatology.T),
        10**6,
        "vvvv",
    )
    return (prediction, week_total.T)


def solution(mesh):
    grid = P(("groups", "member"), "patch", None)
    node = P("patch", None)
    week = P(("groups", "patch"), None)
    return jax.shard_map(
        shards,
        mesh=mesh,
        in_specs=(grid,) + (P(),) * 14 + (node,) * 4 + (week,),
        out_specs=(grid, week),
        check_vma=False,
    )
```

```python
import functools

import jax
import jax.numpy as jnp
from jax import lax
from jax.experimental import pallas as pl
from jax.experimental.pallas import tpu as pltpu
from jax.sharding import PartitionSpec as P

REACH = 32
GRIM = 128
MHALO = 2 * REACH
EMPTY = -4096
F32 = jnp.float32
BF16 = jnp.bfloat16


def dot(a, b):
    return jnp.dot(a, b, preferred_element_type=F32)


def silu(u):
    return u + u * jnp.tanh(u)


def iota(shape, dim):
    return lax.broadcasted_iota(jnp.int32, shape, dim)


def ranks(shape, dim):
    return iota(shape, dim).astype(F32).astype(BF16)


def twice(a):
    return jnp.concatenate([a, a], axis=0)


def wide(a, width):
    return jnp.concatenate([a] * (width // a.shape[1]), axis=1)


def wrap(a, size):
    a = jnp.where(a < 0, a + size, a)
    return jnp.where(a >= size, a - size, a)


def small(idx):
    return idx.astype(F32).astype(BF16)


def marks(idx, height):
    rows = ranks((height, idx.shape[1]), 0)
    return jnp.where(rows == idx, jnp.ones((), BF16), jnp.zeros((), BF16))


def counts(idx, height, base):
    parts = []
    for first in range(0, height, 256):
        size = min(256, height - first)
        near = small(idx - (base + first))
        total = marks(near[0:1], size)
        for slot in range(1, idx.shape[0]):
            total = total + marks(near[slot : slot + 1], size)
        parts.append(total)
    return parts[0] if len(parts) == 1 else jnp.concatenate(parts, axis=0)


def spread(channels, members, member):
    shape = (channels * members, channels)
    return jnp.where(iota(shape, 0) == iota(shape, 1) * members + member, 1.0, 0.0).astype(BF16)


def turned(w, scale):
    return (w.astype(F32) * scale).T.astype(BF16)


def column(b, scale):
    return (jnp.broadcast_to(b, (128, b.shape[1])) * scale).T


def fetch(sources, targets, sems):
    copies = [
        pltpu.make_async_copy(source, target, sems.at[i])
        for i, (source, target) in enumerate(zip(sources, targets))
    ]
    for copy in copies:
        copy.start()
    return copies


def pack_kernel(
    patches,
    place,
    fields_hbm,
    senders_hbm,
    near_hbm,
    x_ref,
    up_ref,
    down_ref,
    k_ref,
    n_ref,
    fields_ref,
    senders_ref,
    near_ref,
    sems,
):
    copies = fetch(
        (fields_hbm, senders_hbm, near_hbm), (fields_ref, senders_ref, near_ref), sems
    )
    for copy in copies:
        copy.wait()
    channels, members, rows = fields_ref.shape
    nodes = senders_ref.shape[1]
    nbrs = near_ref.shape[0]
    stride = rows // nodes
    halo = up_ref.shape[1]
    kx = channels * members
    x = fields_ref[...].reshape(kx, rows)
    x_ref[:kx, :] = x
    x_ref[kx:, :] = jnp.zeros((x_ref.shape[0] - kx, rows), BF16)
    senders = senders_ref[...]
    node = iota(senders.shape, 1)
    k = wrap(senders - place[0] * rows - node * stride + GRIM, rows * patches) - GRIM
    k = jnp.where(senders >= 0, k, EMPTY)
    k = pltpu.roll(k, MHALO, 1)
    k_ref[...] = k
    near = near_ref[...]
    near = wrap(near - place[0] * nodes - iota(near.shape, 1) + REACH, nodes * patches) - REACH
    n_ref[:nbrs, :] = near
    n_ref[nbrs:, :] = jnp.zeros((8 - nbrs, nodes), jnp.int32)
    near = pltpu.roll(n_ref[...], MHALO, 1)
    n_ref[...] = near
    zero = jnp.zeros((8, halo - 3 * 128), F32)
    k = k.astype(F32)[:, :128]
    extra = [k[:8], k[8:], near.astype(F32)[:, :128], zero]
    extra = jnp.concatenate(extra, axis=1).astype(BF16)
    up_ref[...] = jnp.concatenate([x[:, rows - halo :], extra], axis=0)
    down_ref[...] = jnp.concatenate([x[:, :halo], extra], axis=0)


def own_kernel(
    members,
    x_ref,
    k_ref,
    w_embed,
    b_embed,
    w_encode,
    b_encode,
    gain,
    w_receive,
    w_sender,
    b_process,
    w_update,
    w_decmesh,
    w_decgrid,
    b_decode,
    w_output,
    gp_ref,
    edge_ref,
    part_ref,
    embed_t,
    mesh_t,
    out_t,
    encode_t,
    cols_ref,
    wcat,
    bdec,
    h_ref,
    msg_ref,
    count_ref,
):
    channels, hidden = w_embed.shape
    rows = x_ref.shape[1]
    nodes = k_ref.shape[1]
    kx = channels * members
    for m in range(members):
        sp = spread(channels, members, m)
        we = dot(sp, w_embed[...]) * 0.5
        we = jnp.concatenate([we, jnp.zeros((x_ref.shape[0] - kx, hidden), F32)], axis=0)
        embed_t[m * hidden : (m + 1) * hidden, :] = we.T.astype(BF16)
        out_t[:, m * hidden : (m + 1) * hidden] = dot(sp, w_output[...]).astype(BF16)
    enc = turned(w_encode[...], 0.5)
    encode_t[...] = enc
    wcat[:hidden, :] = enc
    wcat[hidden:, :] = turned(w_decgrid[...], 0.5)
    mesh_t[0] = turned(w_sender[...], 0.5)
    mesh_t[1] = turned(w_receive[...], 0.5)
    mesh_t[2] = turned(w_update[...], 1.0)
    mesh_t[3] = turned(w_decmesh[...], 0.5)
    cols_ref[0] = column(b_embed[...], 0.5)
    cols_ref[1] = column(b_encode[...], 0.5)
    cols_ref[2] = column(b_process[...], 0.5)
    cols_ref[3] = column(gain[...], 1.0)
    bdec[...] = column(b_decode[...], 0.5)
    pre = dot(embed_t[...], x_ref[...])
    h_ref[...] = silu((pre + wide(twice(cols_ref[0]), rows)).astype(BF16))
    for m in range(members):
        part = slice(m * hidden, (m + 1) * hidden)
        y = dot(wcat[...], h_ref[part, :])
        msg_ref[part, :] = silu((y[:hidden] + wide(cols_ref[1], rows)).astype(BF16))
        gp_ref[part, :] = (y[hidden:] + wide(bdec[...], rows)).astype(BF16)
    edge_ref[:, :GRIM] = msg_ref[:, :GRIM]
    edge_ref[:, GRIM:] = msg_ref[:, rows - GRIM :]
    stride = rows // nodes
    node = (iota(k_ref.shape, 1) + (nodes - MHALO)) % nodes
    idx = k_ref[...] + node * stride
    for base in range(0, rows, 128):
        near = small(idx - base)
        first = max(0, (base - GRIM - stride) // stride)
        last = min(nodes - 1, (base + 127 + GRIM) // stride)
        touched = {(r + MHALO) % nodes // 128 for r in range(first, last + 1)}
        for tile in range(nodes // 128):
            lanes = slice(128 * tile, 128 * (tile + 1))
            if tile in touched:
                total = marks(near[0:1, lanes], 128)
                for slot in range(1, idx.shape[0]):
                    total = total + marks(near[slot : slot + 1, lanes], 128)
            else:
                total = jnp.zeros((128, 128), BF16)
            count_ref[base : base + 128, lanes] = total
    part_ref[...] = dot(msg_ref[...], count_ref[...])


def rest_kernel(
    members,
    patches,
    place,
    lo_ref,
    hi_ref,
    x_ref,
    k_ref,
    near_ref,
    sent_ref,
    gp_ref,
    edge_ref,
    part_ref,
    embed_t,
    mesh_t,
    out_t,
    encode_t,
    cols_ref,
    bout_ref,
    pred_ref,
    total_ref,
    xh_ref,
    msg_ref,
    sr_ref,
    sum_ref,
    p_ref,
):
    hidden = encode_t.shape[0]
    kx = out_t.shape[0]
    channels = kx // members
    rows = x_ref.shape[1]
    halo = lo_ref.shape[1]
    both = members * hidden
    nodes = k_ref.shape[1]
    top = lo_ref.shape[0]
    xh_ref[:top, :halo] = lo_ref[...]
    xh_ref[:top, halo:] = hi_ref[...]
    xh_ref[top:, :] = jnp.zeros((xh_ref.shape[0] - top, 2 * halo), BF16)
    h = silu((dot(embed_t[...], xh_ref[...]) + wide(twice(cols_ref[0]), 2 * halo)).astype(BF16))
    for m in range(members):
        part = slice(m * hidden, (m + 1) * hidden)
        y = dot(encode_t[...], h[part])
        msg_ref[part, :] = silu((y + wide(cols_ref[1], 2 * halo)).astype(BF16))
    tail = kx // 16 * 16
    lo_x = lo_ref[tail : tail + 16, :].astype(F32)[kx - tail :].astype(jnp.int32)
    hi_x = hi_ref[tail : tail + 16, :].astype(F32)[kx - tail :].astype(jnp.int32)
    slots = jnp.concatenate([lo_x[:, :128], lo_x[:, 128:256]], axis=0)
    lane = iota(slots.shape, 1)
    seam = k_ref[:, :128]
    near_by = lane * 8 + (halo - 8 * MHALO)
    own = near_by + seam
    left = jnp.where(lane < MHALO, near_by + slots, jnp.where(own < halo, own, EMPTY))
    slots = jnp.concatenate([hi_x[:, :128], hi_x[:, 128:256]], axis=0)
    near_by = lane * 8 - (rows - GRIM - 8 * (nodes - MHALO))
    own = near_by + seam
    right = jnp.where(lane >= MHALO, near_by + slots, jnp.where(own >= GRIM, own, EMPTY))
    lsum = dot(msg_ref[:, :halo], counts(left, halo, 0)) + dot(
        edge_ref[:, :GRIM], counts(left, GRIM, halo)
    )
    rsum = dot(edge_ref[:, GRIM:], counts(right, GRIM, 0)) + dot(
        msg_ref[:, halo:], counts(right, halo, GRIM)
    )
    seam = part_ref[:, :128]
    lane = iota(seam.shape, 1)
    lsum = lsum + jnp.where(lane >= MHALO, seam, 0.0)
    rsum = rsum + jnp.where(lane < MHALO, seam, 0.0)
    sums = jnp.concatenate([lsum, part_ref[:, 128:], rsum], axis=1)
    ext = sums.shape[1]
    latents = []
    for m in range(members):
        s = sums[m * hidden : (m + 1) * hidden]
        scale = lax.rsqrt(jnp.sum(s * s, axis=0, keepdims=True) * (1.0 / hidden) + 1e-5)
        latents.append((wide(cols_ref[3], ext) * s * scale).astype(BF16))
    latent = jnp.concatenate(latents, axis=1)
    send = dot(mesh_t[0], latent).astype(BF16)
    recv = (dot(mesh_t[1], latent) + wide(cols_ref[2], members * ext)).astype(BF16)
    for m in range(members):
        sr_ref[m * hidden : (m + 1) * hidden, :] = send[:, m * ext : (m + 1) * ext]
    seam = near_ref[:, :128]
    lane = iota(seam.shape, 1)
    blocks = (
        (jnp.where(lane < MHALO, lo_x[:, 256:384], seam), 0, 256),
        (near_ref[:, 128:], 0, 384),
        (jnp.where(lane >= MHALO, hi_x[:, 256:384], seam), 128, 256),
    )
    sums = []
    for b, (k, first, height) in enumerate(blocks):
        at = k + lane + (128 * b - first)
        base = jnp.concatenate(
            [recv[:, m * ext + 128 * b : m * ext + 128 * (b + 1)] for m in range(members)], axis=0
        )
        total = None
        for j in range(0, 6, 2):
            pair = jnp.concatenate([at[j : j + 1], at[j + 1 : j + 2]], axis=1)
            hot = [marks(small(pair - f), min(256, height - f)) for f in range(0, height, 256)]
            hot = hot[0] if len(hot) == 1 else jnp.concatenate(hot, axis=0)
            got = dot(sr_ref[:, first : first + height], hot).astype(BF16) + wide(base, 256)
            act = silu(got).astype(F32)
            act = act[:, :128] + act[:, 128:]
            total = act if total is None else total + act
        sums.append(total.astype(BF16))
    process = jnp.concatenate(
        [s[m * hidden : (m + 1) * hidden] for m in range(members) for s in sums], axis=1
    )
    new = (latent.astype(F32) + dot(mesh_t[2], process)).astype(BF16)
    part = dot(mesh_t[3], new).astype(BF16)
    for m in range(members):
        sr_ref[m * hidden : (m + 1) * hidden, :] = part[:, m * ext : (m + 1) * ext]
    sent = wrap(sent_ref[...] - place[0] * nodes + MHALO, nodes * patches)
    half = rows // 2
    idx = small(jnp.where(iota(sent.shape, 1) >= half, sent - 128, sent))
    for b in range(2):
        lanes = slice(b * half, (b + 1) * half)
        window = sr_ref[:, 128 * b : 128 * b + 256]
        total = None
        for j in range(idx.shape[0]):
            got = dot(window, marks(idx[j : j + 1, lanes], 256)).astype(BF16)
            act = silu(got + gp_ref[:, lanes])
            total = act if total is None else total + act
        sum_ref[:, lanes] = total
    bout = (iota((kx, channels), 0) // members == iota((kx, channels), 1)).astype(F32)
    bout = jnp.sum(bout * bout_ref[...], axis=1, keepdims=True)
    delta = dot(out_t[...], sum_ref[...]) + bout
    pred = (x_ref[:kx, :].astype(F32) + delta).astype(BF16)
    pred_ref[...] = pred.reshape(channels, members, rows)
    p_ref[:kx, :] = pred
    p_ref[kx:, :] = jnp.zeros((p_ref.shape[0] - kx, rows), BF16)
    shape = (channels, x_ref.shape[0])
    fold = jnp.where(iota(shape, 1) // members == iota(shape, 0), 1.0, 0.0).astype(BF16)
    total_ref[...] = dot(fold, p_ref[...]).astype(BF16)


def week_kernel(count, total_ref, other_ref, week_ref, clim_ref, out_ref):
    ensemble = (total_ref[...].astype(F32) + other_ref[...].astype(F32)) * (1.0 / count)
    out_ref[...] = week_ref[...] + ensemble - clim_ref[...].astype(F32)


def call(kernel, outs, scratch, name, args, flops, spaces, limit=24):
    kinds = {"s": pltpu.SMEM, "v": pltpu.VMEM, "h": pltpu.HBM, "f": pltpu.VMEM}
    args = [
        a if kind in "sf" else pltpu.with_memory_space_constraint(a, kinds[kind])
        for a, kind in zip(args, spaces, strict=True)
    ]
    return pl.pallas_call(
        kernel,
        out_shape=outs,
        in_specs=[pl.BlockSpec(memory_space=kinds[kind]) for kind in spaces],
        out_specs=[pl.BlockSpec(memory_space=pltpu.VMEM)] * len(outs),
        scratch_shapes=scratch,
        name=name,
        compiler_params=pltpu.CompilerParams(vmem_limit_bytes=limit * 1024 * 1024),
        cost_estimate=pl.CostEstimate(flops=flops, bytes_accessed=1 << 22, transcendentals=0),
    )(*args)


def copies_of(args):
    return [pltpu.VMEM(a.shape, a.dtype) for a in args] + [pltpu.SemaphoreType.DMA((len(args),))]


def shards(
    fields,
    w_embed,
    b_embed,
    w_encode,
    b_encode,
    mesh_gain,
    w_receive,
    w_sender,
    b_process,
    w_update,
    w_decmesh,
    w_decgrid,
    b_decode,
    w_output,
    b_output,
    g2m_senders,
    m2g_senders,
    mesh_neighbours,
    climatology,
    week_sum,
):
    members, rows, channels = fields.shape
    hidden = w_encode.shape[0]
    nodes, nbrs = mesh_neighbours.shape
    slots = g2m_senders.shape[1]
    patches = lax.axis_size("patch")
    place = lax.axis_index("patch").astype(jnp.int32).reshape(1)
    kx = members * channels
    kpad = -(-kx // 256) * 256
    halo = MHALO * (rows // nodes) + GRIM
    ext = nodes + 2 * MHALO
    shape = jax.ShapeDtypeStruct
    inside = pltpu.VMEM

    args = (jnp.transpose(fields, (2, 0, 1)), g2m_senders.T, mesh_neighbours.T)
    x, from_low, from_high, k, near = call(
        functools.partial(pack_kernel, patches),
        [
            inside((kpad, rows), BF16),
            inside((kx + 8, halo), BF16),
            inside((kx + 8, halo), BF16),
            inside((slots, nodes), jnp.int32),
            inside((8, nodes), jnp.int32),
        ],
        copies_of(args),
        "pack_halo",
        (place,) + args,
        2 * 10**10,
        "shhh",
    )
    up = [(i, (i + 1) % patches) for i in range(patches)]
    down = [(target, source) for source, target in up]
    lo = lax.ppermute(from_low, "patch", up)
    hi = lax.ppermute(from_high, "patch", down)

    args = (
        w_embed,
        b_embed[None],
        w_encode,
        b_encode[None],
        mesh_gain[None],
        w_receive,
        w_sender,
        b_process[None],
        w_update,
        w_decmesh,
        w_decgrid,
        b_decode[None],
        w_output.T,
    )
    own = call(
        functools.partial(own_kernel, members),
        [
            inside((members * hidden, rows), BF16),
            inside((members * hidden, 2 * GRIM), BF16),
            inside((members * hidden, nodes), F32),
            inside((members * hidden, kpad), BF16),
            inside((4, hidden, hidden), BF16),
            inside((kx, members * hidden), BF16),
            inside((hidden, hidden), BF16),
            inside((4, hidden, 128), F32),
        ],
        [
            pltpu.VMEM((2 * hidden, hidden), BF16),
            pltpu.VMEM((hidden, 128), F32),
            pltpu.VMEM((members * hidden, rows), BF16),
            pltpu.VMEM((members * hidden, rows), BF16),
            pltpu.VMEM((rows, nodes), BF16),
        ],
        "own_rows",
        (x, k) + args,
        10**10,
        "vv" + "f" * len(args),
        32,
    )
    pred, total = call(
        functools.partial(rest_kernel, members, patches),
        [inside((channels, members, rows), BF16), inside((channels, rows), BF16)],
        [
            pltpu.VMEM((kpad, 2 * halo), BF16),
            pltpu.VMEM((members * hidden, 2 * halo), BF16),
            pltpu.VMEM((members * hidden, ext), BF16),
            pltpu.VMEM((members * hidden, rows), BF16),
            pltpu.VMEM((kpad, rows), BF16),
        ],
        "halo_mesh_decode",
        (place, lo, hi, x, k, near, m2g_senders.T) + tuple(own) + (b_output[None],),
        2 * 10**10,
        "s" + "v" * 15,
        32,
    )
    prediction = jnp.transpose(pred, (1, 2, 0))
    other = lax.ppermute(total, "member", [(0, 1), (1, 0)])
    (week_total,) = call(
        functools.partial(week_kernel, members * lax.axis_size("member")),
        [shape((channels, rows), F32)],
        [],
        "week",
        (total, other, week_sum.T, climatology.T),
        10**6,
        "vvvv",
    )
    return (prediction, week_total.T)


def solution(mesh):
    grid = P(("groups", "member"), "patch", None)
    node = P("patch", None)
    week = P(("groups", "patch"), None)
    return jax.shard_map(
        shards,
        mesh=mesh,
        in_specs=(grid,) + (P(),) * 14 + (node,) * 4 + (week,),
        out_specs=(grid, week),
        check_vma=False,
    )
```

```python
import functools

import jax
import jax.numpy as jnp
from jax import lax
from jax.experimental import pallas as pl
from jax.experimental.pallas import tpu as pltpu
from jax.sharding import PartitionSpec as P

REACH = 32
GRIM = 128
MHALO = 2 * REACH
EMPTY = -4096
F32 = jnp.float32
BF16 = jnp.bfloat16


def dot(a, b):
    return jnp.dot(a, b, preferred_element_type=F32)


def silu(u):
    return u + u * jnp.tanh(u)


def iota(shape, dim):
    return lax.broadcasted_iota(jnp.int32, shape, dim)


def ranks(shape, dim):
    return iota(shape, dim).astype(F32).astype(BF16)


def twice(a):
    return jnp.concatenate([a, a], axis=0)


def wide(a, width):
    return jnp.concatenate([a] * (width // a.shape[1]), axis=1)


def wrap(a, size):
    a = jnp.where(a < 0, a + size, a)
    return jnp.where(a >= size, a - size, a)


def small(idx):
    return idx.astype(F32).astype(BF16)


def marks(idx, height):
    rows = ranks((height, idx.shape[1]), 0)
    return jnp.where(rows == idx, jnp.ones((), BF16), jnp.zeros((), BF16))


def counts(idx, height, base):
    parts = []
    for first in range(0, height, 256):
        size = min(256, height - first)
        near = small(idx - (base + first))
        total = marks(near[0:1], size)
        for slot in range(1, idx.shape[0]):
            total = total + marks(near[slot : slot + 1], size)
        parts.append(total)
    return parts[0] if len(parts) == 1 else jnp.concatenate(parts, axis=0)


def spread(channels, members, member):
    shape = (channels * members, channels)
    return jnp.where(iota(shape, 0) == iota(shape, 1) * members + member, 1.0, 0.0).astype(BF16)


def turned(w, scale):
    return (w.astype(F32) * scale).T.astype(BF16)


def column(b, scale):
    return (jnp.broadcast_to(b, (128, b.shape[1])) * scale).T


def fetch(sources, targets, sems):
    copies = [
        pltpu.make_async_copy(source, target, sems.at[i])
        for i, (source, target) in enumerate(zip(sources, targets))
    ]
    for copy in copies:
        copy.start()
    return copies


def pack_kernel(
    patches,
    place,
    fields_hbm,
    senders_hbm,
    near_hbm,
    x_ref,
    up_ref,
    down_ref,
    k_ref,
    n_ref,
    fields_ref,
    senders_ref,
    near_ref,
    sems,
):
    channels, members, rows = fields_ref.shape
    kx = channels * members
    count = sems.shape[0] - 2
    cuts = [channels * i // count for i in range(count + 1)]
    cuts = [slice(a, b) for a, b in zip(cuts, cuts[1:])]
    copies = fetch(
        [senders_hbm, near_hbm] + [fields_hbm.at[cut] for cut in cuts],
        [senders_ref, near_ref] + [fields_ref.at[cut] for cut in cuts],
        sems,
    )
    for copy in copies[:2]:
        copy.wait()
    nodes = senders_ref.shape[1]
    nbrs = near_ref.shape[0]
    stride = rows // nodes
    halo = up_ref.shape[1]
    senders = senders_ref[...]
    node = iota(senders.shape, 1)
    k = wrap(senders - place[0] * rows - node * stride + GRIM, rows * patches) - GRIM
    k = jnp.where(senders >= 0, k, EMPTY)
    k = pltpu.roll(k, MHALO, 1)
    k_ref[...] = k
    near = near_ref[...]
    near = wrap(near - place[0] * nodes - iota(near.shape, 1) + REACH, nodes * patches) - REACH
    n_ref[:nbrs, :] = near
    n_ref[nbrs:, :] = jnp.zeros((8 - nbrs, nodes), jnp.int32)
    near = pltpu.roll(n_ref[...], MHALO, 1)
    n_ref[...] = near
    zero = jnp.zeros((8, halo - 3 * 128), F32)
    k = k.astype(F32)[:, :128]
    extra = [k[:8], k[8:], near.astype(F32)[:, :128], zero]
    extra = jnp.concatenate(extra, axis=1).astype(BF16)
    for copy in copies[2:]:
        copy.wait()
    x = fields_ref[...].reshape(kx, rows)
    x_ref[:kx, :] = x
    x_ref[kx:, :] = jnp.zeros((x_ref.shape[0] - kx, rows), BF16)
    up_ref[...] = jnp.concatenate([x[:, rows - halo :], extra], axis=0)
    down_ref[...] = jnp.concatenate([x[:, :halo], extra], axis=0)


def embed_rows(members, x_ref, w_embed, b_embed, h_ref, embed_t, col_ref):
    channels, hidden = w_embed.shape
    rows = x_ref.shape[1]
    kx = channels * members
    for m in range(members):
        sp = spread(channels, members, m)
        we = dot(sp, w_embed[...]) * 0.5
        we = jnp.concatenate([we, jnp.zeros((x_ref.shape[0] - kx, hidden), F32)], axis=0)
        embed_t[m * hidden : (m + 1) * hidden, :] = we.T.astype(BF16)
    col_ref[...] = column(b_embed[...], 0.5)
    pre = dot(embed_t[...], x_ref[...])
    h_ref[...] = silu((pre + wide(twice(col_ref[...]), rows)).astype(BF16))


def own_counts(k_ref, count_ref):
    rows, nodes = count_ref.shape
    stride = rows // nodes
    node = (iota(k_ref.shape, 1) + (nodes - MHALO)) % nodes
    idx = k_ref[...] + node * stride
    for base in range(0, rows, 128):
        near = small(idx - base)
        first = max(0, (base - GRIM - stride) // stride)
        last = min(nodes - 1, (base + 127 + GRIM) // stride)
        touched = {(r + MHALO) % nodes // 128 for r in range(first, last + 1)}
        for tile in range(nodes // 128):
            lanes = slice(128 * tile, 128 * (tile + 1))
            if tile in touched:
                total = marks(near[0:1, lanes], 128)
                for slot in range(1, idx.shape[0]):
                    total = total + marks(near[slot : slot + 1, lanes], 128)
            else:
                total = jnp.zeros((128, 128), BF16)
            count_ref[base : base + 128, lanes] = total


def early_kernel(members, place, down_in, x_ref, w_embed, b_embed, down_ref, *outs):
    del down_in, down_ref

    @pl.when(place[0] == 0)
    def _():
        embed_rows(members, x_ref, w_embed, b_embed, *outs)


def own_kernel(members, place, x_ref, w_embed, b_embed, *refs):
    k_ref, w_encode, w_decgrid = refs[3:6]
    b_encode, gain, w_receive, w_sender, b_process, w_update, w_decmesh, b_decode, w_output = refs[6:15]
    early = refs[15:18]
    gp_ref, edge_ref, part_ref, mesh_t, out_t, cols_ref, wcat, msg_ref, count_ref = refs[18:]
    h_ref = early[0]

    @pl.when(place[0] != 0)
    def _():
        embed_rows(members, x_ref, w_embed, b_embed, *early)

    own_counts(k_ref, count_ref)
    hidden = w_update.shape[0]
    rows = h_ref.shape[1]
    channels = w_output.shape[0]
    wcat[:hidden, :] = turned(w_encode[...], 0.5)
    wcat[hidden:, :] = turned(w_decgrid[...], 0.5)
    cols_ref[0] = column(b_encode[...], 0.5)
    cols_ref[1] = column(b_process[...], 0.5)
    cols_ref[2] = column(gain[...], 1.0)
    cols_ref[3] = column(b_decode[...], 0.5)
    for m in range(members):
        part = slice(m * hidden, (m + 1) * hidden)
        y = dot(wcat[...], h_ref[part, :])
        msg_ref[part, :] = silu((y[:hidden] + wide(cols_ref[0], rows)).astype(BF16))
        gp_ref[part, :] = (y[hidden:] + wide(cols_ref[3], rows)).astype(BF16)
    edge_ref[:, :GRIM] = msg_ref[:, :GRIM]
    edge_ref[:, GRIM:] = msg_ref[:, rows - GRIM :]
    part_ref[...] = dot(msg_ref[...], count_ref[...])
    for m in range(members):
        sp = spread(channels, members, m)
        out_t[:, m * hidden : (m + 1) * hidden] = dot(sp, w_output[...]).astype(BF16)
    mesh_t[0] = turned(w_sender[...], 0.5)
    mesh_t[1] = turned(w_receive[...], 0.5)
    mesh_t[2] = turned(w_update[...], 1.0)
    mesh_t[3] = turned(w_decmesh[...], 0.5)


def halo_messages(members, embed_t, wcat, col_ref, cols_ref, xh_ref, halo_ref, msg_ref):
    hidden = wcat.shape[1]
    top, halo = halo_ref.shape
    xh_ref[:top, :] = halo_ref[...]
    xh_ref[top:, :] = jnp.zeros((xh_ref.shape[0] - top, halo), BF16)
    h = silu((dot(embed_t[...], xh_ref[...]) + wide(twice(col_ref[...]), halo)).astype(BF16))
    for m in range(members):
        part = slice(m * hidden, (m + 1) * hidden)
        y = dot(wcat[:hidden, :], h[part])
        msg_ref[part, :] = silu((y + wide(cols_ref[0], halo)).astype(BF16))


def offsets(halo_ref):
    tail = halo_ref.shape[0] - 16
    sent = halo_ref[tail:, :].astype(F32)[8:].astype(jnp.int32)
    return jnp.concatenate([sent[:, :128], sent[:, 128:256]], axis=0), sent[:, 256:384]


def latent_rows(members, sums, gain):
    hidden = sums.shape[0] // members
    latents = []
    for m in range(members):
        s = sums[m * hidden : (m + 1) * hidden]
        scale = lax.rsqrt(jnp.sum(s * s, axis=0, keepdims=True) * (1.0 / hidden) + 1e-5)
        latents.append((wide(gain, sums.shape[1]) * s * scale).astype(BF16))
    return jnp.concatenate(latents, axis=1)


def stacked(members, a):
    lanes = a.shape[1] // members
    return jnp.concatenate([a[:, m * lanes : (m + 1) * lanes] for m in range(members)], axis=0)


def process_sum(window, at, base):
    height = window.shape[1]
    total = None
    for j in range(0, 6, 2):
        pair = jnp.concatenate([at[j : j + 1], at[j + 1 : j + 2]], axis=1)
        hot = [marks(small(pair - f), min(256, height - f)) for f in range(0, height, 256)]
        hot = hot[0] if len(hot) == 1 else jnp.concatenate(hot, axis=0)
        got = dot(window, hot).astype(BF16) + wide(base, 256)
        act = silu(got).astype(F32)
        act = act[:, :128] + act[:, 128:]
        total = act if total is None else total + act
    return total.astype(BF16)


def left_kernel(
    members,
    lo_ref,
    k_ref,
    near_ref,
    embed_t,
    col_ref,
    edge_ref,
    part_ref,
    mesh_t,
    cols_ref,
    wcat,
    latent_ref,
    send_ref,
    recv_ref,
    proc_ref,
    xh_ref,
    msg_ref,
):
    halo = lo_ref.shape[1]
    halo_messages(members, embed_t, wcat, col_ref, cols_ref, xh_ref, lo_ref, msg_ref)
    slots, lo_near = offsets(lo_ref)
    lane = iota(slots.shape, 1)
    near_by = lane * 8 + (halo - 8 * MHALO)
    own = near_by + k_ref[:, :128]
    left = jnp.where(lane < MHALO, near_by + slots, jnp.where(own < halo, own, EMPTY))
    lsum = dot(msg_ref[...], counts(left, halo, 0)) + dot(
        edge_ref[:, :GRIM], counts(left, GRIM, halo)
    )
    seam = part_ref[:, :128]
    lsum = lsum + jnp.where(iota(seam.shape, 1) >= MHALO, seam, 0.0)
    sums = jnp.concatenate([lsum, part_ref[:, 128:]], axis=1)
    latent = latent_rows(members, sums, cols_ref[2])
    latent_ref[...] = latent
    send_ref[...] = stacked(members, dot(mesh_t[0], latent).astype(BF16))
    recv = (dot(mesh_t[1], latent) + wide(cols_ref[1], latent.shape[1])).astype(BF16)
    recv_ref[...] = stacked(members, recv)
    seam = near_ref[:, :128]
    lane = iota(seam.shape, 1)
    at = jnp.where(lane < MHALO, lo_near, seam) + lane
    proc_ref[...] = process_sum(send_ref[...], at, recv_ref[:, :128])


def rest_kernel(
    members,
    patches,
    place,
    hi_ref,
    x_ref,
    k_ref,
    near_ref,
    sent_ref,
    embed_t,
    col_ref,
    gp_ref,
    edge_ref,
    part_ref,
    mesh_t,
    out_t,
    cols_ref,
    wcat,
    latent_ref,
    send_ref,
    recv_ref,
    proc_ref,
    bout_ref,
    pred_ref,
    total_ref,
    xh_ref,
    msg_ref,
    sr_ref,
    sum_ref,
    p_ref,
):
    hidden = wcat.shape[1]
    kx = out_t.shape[0]
    channels = kx // members
    rows = x_ref.shape[1]
    halo = hi_ref.shape[1]
    nodes = k_ref.shape[1]
    halo_messages(members, embed_t, wcat, col_ref, cols_ref, xh_ref, hi_ref, msg_ref)
    slots, hi_near = offsets(hi_ref)
    lane = iota(slots.shape, 1)
    near_by = lane * 8 - (rows - GRIM - 8 * (nodes - MHALO))
    own = near_by + k_ref[:, :128]
    right = jnp.where(lane >= MHALO, near_by + slots, jnp.where(own >= GRIM, own, EMPTY))
    rsum = dot(edge_ref[:, GRIM:], counts(right, GRIM, 0)) + dot(
        msg_ref[...], counts(right, halo, GRIM)
    )
    seam = part_ref[:, :128]
    rsum = rsum + jnp.where(iota(seam.shape, 1) < MHALO, seam, 0.0)
    latent = latent_rows(members, rsum, cols_ref[2])
    sr_ref[:, :256] = send_ref[...]
    sr_ref[:, 256:] = stacked(members, dot(mesh_t[0], latent).astype(BF16))
    recv = (dot(mesh_t[1], latent) + wide(cols_ref[1], latent.shape[1])).astype(BF16)
    seam = near_ref[:, :128]
    lane = iota(seam.shape, 1)
    mid = process_sum(sr_ref[...], near_ref[:, 128:] + lane + 128, recv_ref[:, 128:])
    at = jnp.where(lane >= MHALO, hi_near, seam) + lane + 128
    last = process_sum(sr_ref[:, 128:], at, stacked(members, recv))
    sums = [proc_ref[...], mid, last]
    pieces = [s[m * hidden : (m + 1) * hidden] for m in range(members) for s in sums]
    process = jnp.concatenate(pieces, axis=1)
    pieces = []
    for m in range(members):
        pieces.append(latent_ref[:, 256 * m : 256 * (m + 1)])
        pieces.append(latent[:, 128 * m : 128 * (m + 1)])
    latent = jnp.concatenate(pieces, axis=1)
    new = (latent.astype(F32) + dot(mesh_t[2], process)).astype(BF16)
    sr_ref[...] = stacked(members, dot(mesh_t[3], new).astype(BF16))
    sent = wrap(sent_ref[...] - place[0] * nodes + MHALO, nodes * patches)
    half = rows // 2
    idx = small(jnp.where(iota(sent.shape, 1) >= half, sent - 128, sent))
    for b in range(2):
        lanes = slice(b * half, (b + 1) * half)
        window = sr_ref[:, 128 * b : 128 * b + 256]
        total = None
        for j in range(idx.shape[0]):
            got = dot(window, marks(idx[j : j + 1, lanes], 256)).astype(BF16)
            act = silu(got + gp_ref[:, lanes])
            total = act if total is None else total + act
        sum_ref[:, lanes] = total
    bout = (iota((kx, channels), 0) // members == iota((kx, channels), 1)).astype(F32)
    bout = jnp.sum(bout * bout_ref[...], axis=1, keepdims=True)
    delta = dot(out_t[...], sum_ref[...]) + bout
    pred = (x_ref[:kx, :].astype(F32) + delta).astype(BF16)
    pred_ref[...] = pred.reshape(channels, members, rows)
    p_ref[:kx, :] = pred
    p_ref[kx:, :] = jnp.zeros((p_ref.shape[0] - kx, rows), BF16)
    shape = (channels, x_ref.shape[0])
    fold = jnp.where(iota(shape, 1) // members == iota(shape, 0), 1.0, 0.0).astype(BF16)
    total_ref[...] = dot(fold, p_ref[...]).astype(BF16)


def week_kernel(count, total_ref, other_ref, week_ref, clim_ref, out_ref):
    ensemble = (total_ref[...].astype(F32) + other_ref[...].astype(F32)) * (1.0 / count)
    out_ref[...] = week_ref[...] + ensemble - clim_ref[...].astype(F32)


def call(kernel, outs, scratch, name, args, flops, spaces, limit=24, aliases={}):
    kinds = {"s": pltpu.SMEM, "v": pltpu.VMEM, "h": pltpu.HBM, "f": pltpu.VMEM}
    args = [
        a if kind in "sf" else pltpu.with_memory_space_constraint(a, kinds[kind])
        for a, kind in zip(args, spaces, strict=True)
    ]
    return pl.pallas_call(
        kernel,
        out_shape=outs,
        in_specs=[pl.BlockSpec(memory_space=kinds[kind]) for kind in spaces],
        out_specs=[pl.BlockSpec(memory_space=pltpu.VMEM)] * len(outs),
        scratch_shapes=scratch,
        name=name,
        input_output_aliases=aliases,
        compiler_params=pltpu.CompilerParams(vmem_limit_bytes=limit * 1024 * 1024),
        cost_estimate=pl.CostEstimate(flops=flops, bytes_accessed=1 << 22, transcendentals=0),
    )(*args)


def shards(
    fields,
    w_embed,
    b_embed,
    w_encode,
    b_encode,
    mesh_gain,
    w_receive,
    w_sender,
    b_process,
    w_update,
    w_decmesh,
    w_decgrid,
    b_decode,
    w_output,
    b_output,
    g2m_senders,
    m2g_senders,
    mesh_neighbours,
    climatology,
    week_sum,
):
    members, rows, channels = fields.shape
    hidden = w_encode.shape[0]
    nodes, nbrs = mesh_neighbours.shape
    slots = g2m_senders.shape[1]
    patches = lax.axis_size("patch")
    place = lax.axis_index("patch").astype(jnp.int32).reshape(1)
    kx = members * channels
    kpad = -(-kx // 256) * 256
    halo = MHALO * (rows // nodes) + GRIM
    ext = nodes + 2 * MHALO
    shape = jax.ShapeDtypeStruct
    inside = pltpu.VMEM

    args = (jnp.transpose(fields, (2, 0, 1)), g2m_senders.T, mesh_neighbours.T)
    x, from_low, from_high, k, near = call(
        functools.partial(pack_kernel, patches),
        [
            inside((kpad, rows), BF16),
            inside((kx + 8, halo), BF16),
            inside((kx + 8, halo), BF16),
            inside((slots, nodes), jnp.int32),
            inside((8, nodes), jnp.int32),
        ],
        [pltpu.VMEM(a.shape, a.dtype) for a in args] + [pltpu.SemaphoreType.DMA((3,))],
        "pack_halo",
        (place,) + args,
        2 * 10**10,
        "shhh",
    )
    up = [(i, (i + 1) % patches) for i in range(patches)]
    down = [(target, source) for source, target in up]
    lo = lax.ppermute(from_low, "patch", up)
    embedded = [
        inside((members * hidden, rows), BF16),
        inside((members * hidden, kpad), BF16),
        inside((hidden, 128), F32),
    ]
    args = (x, w_embed, b_embed[None])
    from_high, *early = call(
        functools.partial(early_kernel, members),
        [inside((kx + 8, halo), BF16)] + embedded,
        [],
        "embed_early",
        (place, from_high) + args,
        10**10,
        "svvff",
        20,
        {1: 0},
    )
    hi = lax.ppermute(from_high, "patch", down)
    own = call(
        functools.partial(own_kernel, members),
        embedded
        + [
            inside((members * hidden, rows), BF16),
            inside((members * hidden, 2 * GRIM), BF16),
            inside((members * hidden, nodes), F32),
            inside((4, hidden, hidden), BF16),
            inside((kx, members * hidden), BF16),
            inside((4, hidden, 128), F32),
            inside((2 * hidden, hidden), BF16),
        ],
        [pltpu.VMEM((members * hidden, rows), BF16), pltpu.VMEM((rows, nodes), BF16)],
        "own_rows",
        (place,)
        + args
        + tuple(early)
        + (
            k,
            w_encode,
            w_decgrid,
            b_encode[None],
            mesh_gain[None],
            w_receive,
            w_sender,
            b_process[None],
            w_update,
            w_decmesh,
            b_decode[None],
            w_output.T,
        ),
        10**10,
        "svff" + "vvv" + "v" + "f" * 11,
        28,
        {4 + i: i for i in range(3)},
    )
    embed_t, col = own[1:3]
    own = own[3:]
    gp, edge, part, mesh_t, out_t, cols, wcat = own
    halo_scratch = [pltpu.VMEM((kpad, halo), BF16), pltpu.VMEM((members * hidden, halo), BF16)]
    left = call(
        functools.partial(left_kernel, members),
        [
            inside((hidden, members * 256), BF16),
            inside((members * hidden, 256), BF16),
            inside((members * hidden, 256), BF16),
            inside((members * hidden, 128), BF16),
        ],
        halo_scratch,
        "low_side",
        (lo, k, near, embed_t, col, edge, part, mesh_t, cols, wcat),
        10**10,
        "v" * 10,
        20,
    )
    pred, total = call(
        functools.partial(rest_kernel, members, patches),
        [inside((channels, members, rows), BF16), inside((channels, rows), BF16)],
        halo_scratch
        + [
            pltpu.VMEM((members * hidden, ext), BF16),
            pltpu.VMEM((members * hidden, rows), BF16),
            pltpu.VMEM((kpad, rows), BF16),
        ],
        "high_side_decode",
        (place, hi, x, k, near, m2g_senders.T, embed_t, col)
        + tuple(own)
        + tuple(left)
        + (b_output[None],),
        2 * 10**10,
        "s" + "v" * 19,
        32,
    )
    prediction = jnp.transpose(pred, (1, 2, 0))
    other = lax.ppermute(total, "member", [(0, 1), (1, 0)])
    (week_total,) = call(
        functools.partial(week_kernel, members * lax.axis_size("member")),
        [shape((channels, rows), F32)],
        [],
        "week",
        (total, other, week_sum.T, climatology.T),
        10**6,
        "vvvv",
    )
    return (prediction, week_total.T)


def solution(mesh):
    grid = P(("groups", "member"), "patch", None)
    node = P("patch", None)
    week = P(("groups", "patch"), None)
    return jax.shard_map(
        shards,
        mesh=mesh,
        in_specs=(grid,) + (P(),) * 14 + (node,) * 4 + (week,),
        out_specs=(grid, week),
        check_vma=False,
    )
```

```python
import functools

import jax
import jax.numpy as jnp
from jax import lax
from jax.experimental import pallas as pl
from jax.experimental.pallas import tpu as pltpu
from jax.sharding import PartitionSpec as P

REACH = 32
GRIM = 128
MHALO = 2 * REACH
EMPTY = -4096
F32 = jnp.float32
BF16 = jnp.bfloat16


def dot(a, b):
    return jnp.dot(a, b, preferred_element_type=F32)


def silu(u):
    return u + u * jnp.tanh(u)


def iota(shape, dim):
    return lax.broadcasted_iota(jnp.int32, shape, dim)


def ranks(shape, dim):
    return iota(shape, dim).astype(F32).astype(BF16)


def twice(a):
    return jnp.concatenate([a, a], axis=0)


def wide(a, width):
    return jnp.concatenate([a] * (width // a.shape[1]), axis=1)


def wrap(a, size):
    a = jnp.where(a < 0, a + size, a)
    return jnp.where(a >= size, a - size, a)


def small(idx):
    return idx.astype(F32).astype(BF16)


def marks(idx, height):
    rows = ranks((height, idx.shape[1]), 0)
    return jnp.where(rows == idx, jnp.ones((), BF16), jnp.zeros((), BF16))


def counts(idx, height, base):
    parts = []
    for first in range(0, height, 256):
        size = min(256, height - first)
        near = small(idx - (base + first))
        total = marks(near[0:1], size)
        for slot in range(1, idx.shape[0]):
            total = total + marks(near[slot : slot + 1], size)
        parts.append(total)
    return parts[0] if len(parts) == 1 else jnp.concatenate(parts, axis=0)


def spread(channels, members, member):
    shape = (channels * members, channels)
    return jnp.where(iota(shape, 0) == iota(shape, 1) * members + member, 1.0, 0.0).astype(BF16)


def turned(w, scale):
    return (w.astype(F32) * scale).T.astype(BF16)


def column(b, scale):
    return (jnp.broadcast_to(b, (128, b.shape[1])) * scale).T


def fetch(sources, targets, sems):
    copies = [
        pltpu.make_async_copy(source, target, sems.at[i])
        for i, (source, target) in enumerate(zip(sources, targets))
    ]
    for copy in copies:
        copy.start()
    return copies


def pack_kernel(
    patches,
    place,
    fields_hbm,
    senders_hbm,
    near_hbm,
    x_ref,
    up_ref,
    down_ref,
    k_ref,
    n_ref,
    fields_ref,
    senders_ref,
    near_ref,
    sems,
):
    channels, members, rows = fields_ref.shape
    kx = channels * members
    count = sems.shape[0] - 2
    cuts = [channels * i // count for i in range(count + 1)]
    cuts = [slice(a, b) for a, b in zip(cuts, cuts[1:])]
    copies = fetch(
        [senders_hbm, near_hbm] + [fields_hbm.at[cut] for cut in cuts],
        [senders_ref, near_ref] + [fields_ref.at[cut] for cut in cuts],
        sems,
    )
    for copy in copies[:2]:
        copy.wait()
    nodes = senders_ref.shape[1]
    nbrs = near_ref.shape[0]
    stride = rows // nodes
    halo = up_ref.shape[1]
    senders = senders_ref[...]
    node = iota(senders.shape, 1)
    k = wrap(senders - place[0] * rows - node * stride + GRIM, rows * patches) - GRIM
    k = jnp.where(senders >= 0, k, EMPTY)
    k = pltpu.roll(k, MHALO, 1)
    k_ref[...] = k
    near = near_ref[...]
    near = wrap(near - place[0] * nodes - iota(near.shape, 1) + REACH, nodes * patches) - REACH
    n_ref[:nbrs, :] = near
    n_ref[nbrs:, :] = jnp.zeros((8 - nbrs, nodes), jnp.int32)
    near = pltpu.roll(n_ref[...], MHALO, 1)
    n_ref[...] = near
    zero = jnp.zeros((8, halo - 3 * 128), F32)
    k = k.astype(F32)[:, :128]
    extra = [k[:8], k[8:], near.astype(F32)[:, :128], zero]
    extra = jnp.concatenate(extra, axis=1).astype(BF16)
    for copy in copies[2:]:
        copy.wait()
    x = fields_ref[...].reshape(kx, rows)
    x_ref[:kx, :] = x
    x_ref[kx:, :] = jnp.zeros((x_ref.shape[0] - kx, rows), BF16)
    up_ref[...] = jnp.concatenate([x[:, rows - halo :], extra], axis=0)
    down_ref[...] = jnp.concatenate([x[:, :halo], extra], axis=0)


def embed_rows(members, x_ref, w_embed, b_embed, h_ref, embed_t, col_ref):
    channels, hidden = w_embed.shape
    rows = x_ref.shape[1]
    kx = channels * members
    for m in range(members):
        sp = spread(channels, members, m)
        we = dot(sp, w_embed[...]) * 0.5
        we = jnp.concatenate([we, jnp.zeros((x_ref.shape[0] - kx, hidden), F32)], axis=0)
        embed_t[m * hidden : (m + 1) * hidden, :] = we.T.astype(BF16)
    col_ref[...] = column(b_embed[...], 0.5)
    pre = dot(embed_t[...], x_ref[...])
    h_ref[...] = silu((pre + wide(twice(col_ref[...]), rows)).astype(BF16))


def own_counts(k_ref, count_ref):
    rows, nodes = count_ref.shape
    stride = rows // nodes
    node = (iota(k_ref.shape, 1) + (nodes - MHALO)) % nodes
    idx = k_ref[...] + node * stride
    for base in range(0, rows, 128):
        near = small(idx - base)
        first = max(0, (base - GRIM - stride) // stride)
        last = min(nodes - 1, (base + 127 + GRIM) // stride)
        touched = {(r + MHALO) % nodes // 128 for r in range(first, last + 1)}
        for tile in range(nodes // 128):
            lanes = slice(128 * tile, 128 * (tile + 1))
            if tile in touched:
                total = marks(near[0:1, lanes], 128)
                for slot in range(1, idx.shape[0]):
                    total = total + marks(near[slot : slot + 1, lanes], 128)
            else:
                total = jnp.zeros((128, 128), BF16)
            count_ref[base : base + 128, lanes] = total


def early_kernel(members, place, down_in, x_ref, w_embed, b_embed, down_ref, *outs):
    del down_in, down_ref

    @pl.when(place[0] == 0)
    def _():
        embed_rows(members, x_ref, w_embed, b_embed, *outs)


def own_kernel(members, place, x_ref, w_embed, b_embed, *refs):
    k_ref, w_encode, w_decgrid = refs[3:6]
    b_encode, gain, w_receive, w_sender, b_process, w_update, w_decmesh, b_decode, w_output = refs[6:15]
    early = refs[15:18]
    gp_ref, edge_ref, part_ref, mesh_t, out_t, cols_ref, wcat, msg_ref, count_ref = refs[18:]
    h_ref = early[0]

    @pl.when(place[0] != 0)
    def _():
        embed_rows(members, x_ref, w_embed, b_embed, *early)

    hidden = w_update.shape[0]
    rows = h_ref.shape[1]
    channels = w_output.shape[0]
    wcat[:hidden, :] = turned(w_encode[...], 0.5)
    wcat[hidden:, :] = turned(w_decgrid[...], 0.5)
    cols_ref[0] = column(b_encode[...], 0.5)
    cols_ref[1] = column(b_process[...], 0.5)
    cols_ref[2] = column(gain[...], 1.0)
    cols_ref[3] = column(b_decode[...], 0.5)
    for m in range(members):
        part = slice(m * hidden, (m + 1) * hidden)
        y = dot(wcat[...], h_ref[part, :])
        mesh_t[2 * m] = turned((w_sender, w_update)[m][...], (0.5, 1.0)[m])
        mesh_t[2 * m + 1] = turned((w_receive, w_decmesh)[m][...], 0.5)
        msg_ref[part, :] = silu((y[:hidden] + wide(cols_ref[0], rows)).astype(BF16))
        gp_ref[part, :] = (y[hidden:] + wide(cols_ref[3], rows)).astype(BF16)
    edge_ref[:, :GRIM] = msg_ref[:, :GRIM]
    edge_ref[:, GRIM:] = msg_ref[:, rows - GRIM :]
    own_counts(k_ref, count_ref)
    part_ref[...] = dot(msg_ref[...], count_ref[...])
    for m in range(members):
        sp = spread(channels, members, m)
        out_t[:, m * hidden : (m + 1) * hidden] = dot(sp, w_output[...]).astype(BF16)


def halo_messages(members, embed_t, wcat, col_ref, cols_ref, xh_ref, halo_ref, msg_ref):
    hidden = wcat.shape[1]
    top, halo = halo_ref.shape
    xh_ref[:top, :] = halo_ref[...]
    xh_ref[top:, :] = jnp.zeros((xh_ref.shape[0] - top, halo), BF16)
    h = silu((dot(embed_t[...], xh_ref[...]) + wide(twice(col_ref[...]), halo)).astype(BF16))
    for m in range(members):
        part = slice(m * hidden, (m + 1) * hidden)
        y = dot(wcat[:hidden, :], h[part])
        msg_ref[part, :] = silu((y + wide(cols_ref[0], halo)).astype(BF16))


def offsets(halo_ref):
    tail = halo_ref.shape[0] - 16
    sent = halo_ref[tail:, :].astype(F32)[8:].astype(jnp.int32)
    return jnp.concatenate([sent[:, :128], sent[:, 128:256]], axis=0), sent[:, 256:384]


def latent_rows(members, sums, gain):
    hidden = sums.shape[0] // members
    latents = []
    for m in range(members):
        s = sums[m * hidden : (m + 1) * hidden]
        scale = lax.rsqrt(jnp.sum(s * s, axis=0, keepdims=True) * (1.0 / hidden) + 1e-5)
        latents.append((wide(gain, sums.shape[1]) * s * scale).astype(BF16))
    return jnp.concatenate(latents, axis=1)


def stacked(members, a):
    lanes = a.shape[1] // members
    return jnp.concatenate([a[:, m * lanes : (m + 1) * lanes] for m in range(members)], axis=0)


def process_sum(window, at, base):
    height = window.shape[1]
    total = None
    for j in range(0, 6, 2):
        pair = jnp.concatenate([at[j : j + 1], at[j + 1 : j + 2]], axis=1)
        hot = [marks(small(pair - f), min(256, height - f)) for f in range(0, height, 256)]
        hot = hot[0] if len(hot) == 1 else jnp.concatenate(hot, axis=0)
        got = dot(window, hot).astype(BF16) + wide(base, 256)
        act = silu(got).astype(F32)
        act = act[:, :128] + act[:, 128:]
        total = act if total is None else total + act
    return total.astype(BF16)


def left_kernel(
    members,
    lo_ref,
    k_ref,
    near_ref,
    embed_t,
    col_ref,
    edge_ref,
    part_ref,
    mesh_t,
    cols_ref,
    wcat,
    latent_ref,
    send_ref,
    recv_ref,
    proc_ref,
    xh_ref,
    msg_ref,
):
    halo = lo_ref.shape[1]
    halo_messages(members, embed_t, wcat, col_ref, cols_ref, xh_ref, lo_ref, msg_ref)
    slots, lo_near = offsets(lo_ref)
    lane = iota(slots.shape, 1)
    near_by = lane * 8 + (halo - 8 * MHALO)
    own = near_by + k_ref[:, :128]
    left = jnp.where(lane < MHALO, near_by + slots, jnp.where(own < halo, own, EMPTY))
    lsum = dot(msg_ref[...], counts(left, halo, 0)) + dot(
        edge_ref[:, :GRIM], counts(left, GRIM, halo)
    )
    seam = part_ref[:, :128]
    lsum = lsum + jnp.where(iota(seam.shape, 1) >= MHALO, seam, 0.0)
    sums = jnp.concatenate([lsum, part_ref[:, 128:]], axis=1)
    latent = latent_rows(members, sums, cols_ref[2])
    latent_ref[...] = latent
    send_ref[...] = stacked(members, dot(mesh_t[0], latent).astype(BF16))
    recv = (dot(mesh_t[1], latent) + wide(cols_ref[1], latent.shape[1])).astype(BF16)
    recv_ref[...] = stacked(members, recv)
    seam = near_ref[:, :128]
    lane = iota(seam.shape, 1)
    at = jnp.where(lane < MHALO, lo_near, seam) + lane
    proc_ref[...] = process_sum(send_ref[...], at, recv_ref[:, :128])


def rest_kernel(
    members,
    patches,
    place,
    hi_ref,
    x_ref,
    k_ref,
    near_ref,
    sent_ref,
    embed_t,
    col_ref,
    gp_ref,
    edge_ref,
    part_ref,
    mesh_t,
    out_t,
    cols_ref,
    wcat,
    latent_ref,
    send_ref,
    recv_ref,
    proc_ref,
    bout_ref,
    pred_ref,
    total_ref,
    xh_ref,
    msg_ref,
    sr_ref,
    sum_ref,
    p_ref,
):
    hidden = wcat.shape[1]
    kx = out_t.shape[0]
    channels = kx // members
    rows = x_ref.shape[1]
    halo = hi_ref.shape[1]
    nodes = k_ref.shape[1]
    halo_messages(members, embed_t, wcat, col_ref, cols_ref, xh_ref, hi_ref, msg_ref)
    slots, hi_near = offsets(hi_ref)
    lane = iota(slots.shape, 1)
    near_by = lane * 8 - (rows - GRIM - 8 * (nodes - MHALO))
    own = near_by + k_ref[:, :128]
    right = jnp.where(lane >= MHALO, near_by + slots, jnp.where(own >= GRIM, own, EMPTY))
    rsum = dot(edge_ref[:, GRIM:], counts(right, GRIM, 0)) + dot(
        msg_ref[...], counts(right, halo, GRIM)
    )
    seam = part_ref[:, :128]
    rsum = rsum + jnp.where(iota(seam.shape, 1) < MHALO, seam, 0.0)
    latent = latent_rows(members, rsum, cols_ref[2])
    sr_ref[:, :256] = send_ref[...]
    sr_ref[:, 256:] = stacked(members, dot(mesh_t[0], latent).astype(BF16))
    recv = (dot(mesh_t[1], latent) + wide(cols_ref[1], latent.shape[1])).astype(BF16)
    seam = near_ref[:, :128]
    lane = iota(seam.shape, 1)
    mid = process_sum(sr_ref[...], near_ref[:, 128:] + lane + 128, recv_ref[:, 128:])
    at = jnp.where(lane >= MHALO, hi_near, seam) + lane + 128
    last = process_sum(sr_ref[:, 128:], at, stacked(members, recv))
    sums = [proc_ref[...], mid, last]
    pieces = [s[m * hidden : (m + 1) * hidden] for m in range(members) for s in sums]
    process = jnp.concatenate(pieces, axis=1)
    pieces = []
    for m in range(members):
        pieces.append(latent_ref[:, 256 * m : 256 * (m + 1)])
        pieces.append(latent[:, 128 * m : 128 * (m + 1)])
    latent = jnp.concatenate(pieces, axis=1)
    new = (latent.astype(F32) + dot(mesh_t[2], process)).astype(BF16)
    sr_ref[...] = stacked(members, dot(mesh_t[3], new).astype(BF16))
    sent = wrap(sent_ref[...] - place[0] * nodes + MHALO, nodes * patches)
    half = rows // 2
    idx = small(jnp.where(iota(sent.shape, 1) >= half, sent - 128, sent))
    for b in range(2):
        lanes = slice(b * half, (b + 1) * half)
        window = sr_ref[:, 128 * b : 128 * b + 256]
        total = None
        for j in range(idx.shape[0]):
            got = dot(window, marks(idx[j : j + 1, lanes], 256)).astype(BF16)
            act = silu(got + gp_ref[:, lanes])
            total = act if total is None else total + act
        sum_ref[:, lanes] = total
    bout = (iota((kx, channels), 0) // members == iota((kx, channels), 1)).astype(F32)
    bout = jnp.sum(bout * bout_ref[...], axis=1, keepdims=True)
    delta = dot(out_t[...], sum_ref[...]) + bout
    pred = (x_ref[:kx, :].astype(F32) + delta).astype(BF16)
    pred_ref[...] = pred.reshape(channels, members, rows)
    p_ref[:kx, :] = pred
    p_ref[kx:, :] = jnp.zeros((p_ref.shape[0] - kx, rows), BF16)
    shape = (channels, x_ref.shape[0])
    fold = jnp.where(iota(shape, 1) // members == iota(shape, 0), 1.0, 0.0).astype(BF16)
    total_ref[...] = dot(fold, p_ref[...]).astype(BF16)


def week_kernel(count, total_ref, other_ref, week_ref, clim_ref, out_ref):
    ensemble = (total_ref[...].astype(F32) + other_ref[...].astype(F32)) * (1.0 / count)
    out_ref[...] = week_ref[...] + ensemble - clim_ref[...].astype(F32)


def call(kernel, outs, scratch, name, args, flops, spaces, limit=24, aliases={}):
    kinds = {"s": pltpu.SMEM, "v": pltpu.VMEM, "h": pltpu.HBM, "f": pltpu.VMEM}
    args = [
        a if kind in "sf" else pltpu.with_memory_space_constraint(a, kinds[kind])
        for a, kind in zip(args, spaces, strict=True)
    ]
    return pl.pallas_call(
        kernel,
        out_shape=outs,
        in_specs=[pl.BlockSpec(memory_space=kinds[kind]) for kind in spaces],
        out_specs=[pl.BlockSpec(memory_space=pltpu.VMEM)] * len(outs),
        scratch_shapes=scratch,
        name=name,
        input_output_aliases=aliases,
        compiler_params=pltpu.CompilerParams(vmem_limit_bytes=limit * 1024 * 1024),
        cost_estimate=pl.CostEstimate(flops=flops, bytes_accessed=1 << 22, transcendentals=0),
    )(*args)


def shards(
    fields,
    w_embed,
    b_embed,
    w_encode,
    b_encode,
    mesh_gain,
    w_receive,
    w_sender,
    b_process,
    w_update,
    w_decmesh,
    w_decgrid,
    b_decode,
    w_output,
    b_output,
    g2m_senders,
    m2g_senders,
    mesh_neighbours,
    climatology,
    week_sum,
):
    members, rows, channels = fields.shape
    hidden = w_encode.shape[0]
    nodes, nbrs = mesh_neighbours.shape
    slots = g2m_senders.shape[1]
    patches = lax.axis_size("patch")
    place = lax.axis_index("patch").astype(jnp.int32).reshape(1)
    kx = members * channels
    kpad = -(-kx // 256) * 256
    halo = MHALO * (rows // nodes) + GRIM
    ext = nodes + 2 * MHALO
    shape = jax.ShapeDtypeStruct
    inside = pltpu.VMEM

    args = (jnp.transpose(fields, (2, 0, 1)), g2m_senders.T, mesh_neighbours.T)
    x, from_low, from_high, k, near = call(
        functools.partial(pack_kernel, patches),
        [
            inside((kpad, rows), BF16),
            inside((kx + 8, halo), BF16),
            inside((kx + 8, halo), BF16),
            inside((slots, nodes), jnp.int32),
            inside((8, nodes), jnp.int32),
        ],
        [pltpu.VMEM(a.shape, a.dtype) for a in args] + [pltpu.SemaphoreType.DMA((3,))],
        "pack_halo",
        (place,) + args,
        2 * 10**10,
        "shhh",
    )
    up = [(i, (i + 1) % patches) for i in range(patches)]
    down = [(target, source) for source, target in up]
    lo = lax.ppermute(from_low, "patch", up)
    embedded = [
        inside((members * hidden, rows), BF16),
        inside((members * hidden, kpad), BF16),
        inside((hidden, 128), F32),
    ]
    args = (x, w_embed, b_embed[None])
    from_high, *early = call(
        functools.partial(early_kernel, members),
        [inside((kx + 8, halo), BF16)] + embedded,
        [],
        "embed_early",
        (place, from_high) + args,
        10**10,
        "svvff",
        20,
        {1: 0},
    )
    hi = lax.ppermute(from_high, "patch", down)
    own = call(
        functools.partial(own_kernel, members),
        embedded
        + [
            inside((members * hidden, rows), BF16),
            inside((members * hidden, 2 * GRIM), BF16),
            inside((members * hidden, nodes), F32),
            inside((4, hidden, hidden), BF16),
            inside((kx, members * hidden), BF16),
            inside((4, hidden, 128), F32),
            inside((2 * hidden, hidden), BF16),
        ],
        [pltpu.VMEM((members * hidden, rows), BF16), pltpu.VMEM((rows, nodes), BF16)],
        "own_rows",
        (place,)
        + args
        + tuple(early)
        + (
            k,
            w_encode,
            w_decgrid,
            b_encode[None],
            mesh_gain[None],
            w_receive,
            w_sender,
            b_process[None],
            w_update,
            w_decmesh,
            b_decode[None],
            w_output.T,
        ),
        10**10,
        "svff" + "vvv" + "v" + "f" * 11,
        28,
        {4 + i: i for i in range(3)},
    )
    embed_t, col = own[1:3]
    own = own[3:]
    gp, edge, part, mesh_t, out_t, cols, wcat = own
    halo_scratch = [pltpu.VMEM((kpad, halo), BF16), pltpu.VMEM((members * hidden, halo), BF16)]
    left = call(
        functools.partial(left_kernel, members),
        [
            inside((hidden, members * 256), BF16),
            inside((members * hidden, 256), BF16),
            inside((members * hidden, 256), BF16),
            inside((members * hidden, 128), BF16),
        ],
        halo_scratch,
        "low_side",
        (lo, k, near, embed_t, col, edge, part, mesh_t, cols, wcat),
        10**10,
        "v" * 10,
        20,
    )
    pred, total = call(
        functools.partial(rest_kernel, members, patches),
        [inside((channels, members, rows), BF16), inside((channels, rows), BF16)],
        halo_scratch
        + [
            pltpu.VMEM((members * hidden, ext), BF16),
            pltpu.VMEM((members * hidden, rows), BF16),
            pltpu.VMEM((kpad, rows), BF16),
        ],
        "high_side_decode",
        (place, hi, x, k, near, m2g_senders.T, embed_t, col)
        + tuple(own)
        + tuple(left)
        + (b_output[None],),
        2 * 10**10,
        "s" + "v" * 19,
        32,
    )
    prediction = jnp.transpose(pred, (1, 2, 0))
    other = lax.ppermute(total, "member", [(0, 1), (1, 0)])
    (week_total,) = call(
        functools.partial(week_kernel, members * lax.axis_size("member")),
        [shape((channels, rows), F32)],
        [],
        "week",
        (total, other, week_sum.T, climatology.T),
        10**6,
        "vvvv",
    )
    return (prediction, week_total.T)


def solution(mesh):
    grid = P(("groups", "member"), "patch", None)
    node = P("patch", None)
    week = P(("groups", "patch"), None)
    return jax.shard_map(
        shards,
        mesh=mesh,
        in_specs=(grid,) + (P(),) * 14 + (node,) * 4 + (week,),
        out_specs=(grid, week),
        check_vma=False,
    )
```
